32 devices in a mesh: grp: 2 (over y), seq: 4 (over z), sub: 4 (over x, core).
Axes of the slice: x: 2, y: 2, z: 4, core: 2. Of those that a mesh axis runs over, the one named last changes fastest.
Arguments:
- queries: bfloat16 [1024, 4096], P(('grp', 'seq'), 'sub'), parts along dimension 0, may hold values from -6 to 6
- keys: bfloat16 [1024, 1024], P(('grp', 'seq'), 'sub'), parts along dimension 0, may hold values from -6 to 6
- values: bfloat16 [1024, 1024], P(('grp', 'seq'), 'sub'), parts along dimension 0, may hold values from -6 to 6
- output_gradient: bfloat16 [1024, 4096], P(('grp', 'seq'), 'sub'), parts along dimension 0, may hold values from -6 to 6
- doc_tiles: int32 [4], P('grp'), parts along dimension 0, may hold values from 1 to 24, 32 in all
Outputs:
- attended: bfloat16 [1024, 4096], P(('grp', 'seq'), 'sub'), parts along dimension 0
- query_grad: bfloat16 [1024, 4096], P(('grp', 'seq'), 'sub'), parts along dimension 0
- key_gradient: bfloat16 [1024, 1024], P(('grp', 'seq'), 'sub'), parts along dimension 0
- value_gradient: bfloat16 [1024, 1024], P(('grp', 'seq'), 'sub'), parts along dimension 0
The draws below stay inside these ranges and needn't reach their ends.
There are 2 independent parts, one for each index of `grp`. The reference program is written for one: setup_inputs(seed, part) draws one part's arguments, and reference() takes and returns one part's arrays. A program takes and returns all parts, laid end to end along the dimension named above; each array names one. Nothing has to cross between parts.
Inputs may be any that keep to these rules, and one draw needn't show every extreme that they name: `doc_tiles`: the lengths sum to 32.
All inputs are finite; a program needn't handle non-finite values.
Results may differ from the reference program's by a relative error of at most 0.012.
The reference program's roundings to bfloat16 on the way (of `probs` and `score_grad`) count: a program that leaves them out, or rounds other values in their place, can miss the bound.
Values may be sent and summed in bfloat16 or wider, within the bound.
A program may use at most 64 MiB of HBM per device.

```python
import math
import jax
import jax.numpy as jnp
import numpy as np
from jax import lax

QUERY_HEADS = 32
KEY_VALUE_HEADS = 8
HEAD_SIZE = 128
TILE = 16
PACKED_TOKENS = 512
TILES = 32
DOC_MOST = 24
NDOC = 2


def draw_queries(key, part):
    key = jax.random.fold_in(key, 11)
    return jnp.clip(jax.random.normal(key, (PACKED_TOKENS, QUERY_HEADS * HEAD_SIZE), jnp.float32), -6.0, 6.0).astype(jnp.bfloat16)


def draw_keys(key, part):
    key = jax.random.fold_in(key, 23)
    return jnp.clip(jax.random.normal(key, (PACKED_TOKENS, KEY_VALUE_HEADS * HEAD_SIZE), jnp.float32), -6.0, 6.0).astype(jnp.bfloat16)


def block_levels(stream_key, extent, pieces, smallest, high):
    def one(position, shards_of):
        heights = jax.random.uniform(jax.random.fold_in(jax.random.fold_in(stream_key, 6), position), (shards_of,), jnp.float32, smallest / len(pieces), high / len(pieces))
        return jnp.repeat(jnp.exp(heights), extent[position] // shards_of).reshape((-1,) + (1,) * (len(extent) - position - 1))

    loudness = one(*pieces[0])
    for cut in pieces[1:]:
        loudness = loudness * one(*cut)
    return loudness


def split_up(number_of, total, limit, skew):
    weights = [(1 << 20) // math.isqrt(rank ** skew) + 1 for rank in range(2, number_of + 1)]
    surplus, holding = total - limit - (number_of - 1), [1] * (number_of - 1)
    while surplus > 0:
        free = [i for i in range(number_of - 1) if holding[i] < limit]
        whole, budget = sum([weights[i] for i in free]), surplus
        for i in free:
            extra = min(limit - holding[i], max(1, budget * weights[i] // whole), surplus)
            holding[i] = holding[i] + extra
            surplus = surplus - extra
    return np.array([limit] + holding)


def uneven(own_key, number_of, total, most, slope):
    if number_of == 2:
        one = jax.random.randint(own_key, (), max(1, total - most), min(most, total - 1) + 1)
        return jnp.stack([one, total - one])
    tallies = jnp.asarray(split_up(number_of, total, most, slope), jnp.int32)
    twos = (number_of - 1) // 2
    donor, sink = tallies[1:1 + 2 * twos:2], tallies[2:2 + 2 * twos:2]
    slack = jnp.minimum(donor - 1, most - sink)
    passed = jax.random.randint(jax.random.fold_in(own_key, 1), (twos,), 0, 1 << 20) % (slack + 1)
    tallies = tallies.at[1:1 + 2 * twos:2].set(donor - passed).at[2:2 + 2 * twos:2].set(sink + passed)
    return tallies[jax.random.permutation(jax.random.fold_in(own_key, 2), number_of)]


def bell_draw(key, dims, width, most, cuts=(), kind=jnp.bfloat16):
    factor_of = block_levels(key, dims, cuts, -0.22, 0.18) if cuts else 1.0
    values = jax.random.normal(key, dims, jnp.float32) * width * factor_of
    return jnp.minimum(jnp.maximum(values, -most), most).astype(kind)


def setup_inputs(seed: int = 0, part: int = 0) -> dict:
    arg_keys = jax.random.split(jax.random.key(seed), 6)
    part_keys = jax.random.split(jax.random.fold_in(arg_keys[5], part), 6)
    queries = draw_queries(jax.random.fold_in(jax.random.fold_in(arg_keys[5], part), 71), part)
    keys = draw_keys(jax.random.fold_in(jax.random.fold_in(arg_keys[5], part), 71), part)
    values = bell_draw(part_keys[2], (PACKED_TOKENS, KEY_VALUE_HEADS * HEAD_SIZE), 1.0, 6.0, ((0, 4), (1, 4)))
    output_gradient = bell_draw(part_keys[3], (PACKED_TOKENS, QUERY_HEADS * HEAD_SIZE), 1.0, 6.0, ((0, 4), (1, 4)))
    doc_tiles = uneven(part_keys[4], NDOC, TILES, DOC_MOST, 2).astype(jnp.int32)
    return {"queries": queries, "keys": keys, "values": values, "output_gradient": output_gradient, "doc_tiles": doc_tiles}


very_negative = -1.0e30


def reference(queries, keys, values, output_gradient, doc_tiles):
    count_of_tokens = queries.shape[0]
    query_group_width = QUERY_HEADS // KEY_VALUE_HEADS
    score_scale = HEAD_SIZE ** -0.5
    doc_ends = jnp.cumsum(doc_tiles).astype(jnp.int32) * TILE
    begins = doc_ends - doc_tiles.astype(jnp.int32) * TILE
    positions = jnp.arange(count_of_tokens, dtype=jnp.int32)
    inside = begins[None, :] <= positions[:, None]
    first_token = jnp.max(jnp.where(inside, begins[None, :], 0), axis=1).astype(jnp.int32)
    allowed = (positions[None, :] >= first_token[:, None]) & (positions[None, :] <= positions[:, None])
    heads_of_queries = queries.reshape(count_of_tokens, KEY_VALUE_HEADS, query_group_width, HEAD_SIZE).transpose(1, 2, 0, 3)
    gradient_heads = output_gradient.reshape(count_of_tokens, KEY_VALUE_HEADS, query_group_width, HEAD_SIZE).transpose(1, 2, 0, 3)
    heads_of_keys = keys.reshape(count_of_tokens, KEY_VALUE_HEADS, HEAD_SIZE).transpose(1, 0, 2)
    heads_of_values = values.reshape(count_of_tokens, KEY_VALUE_HEADS, HEAD_SIZE).transpose(1, 0, 2)

    def per_group(group_args):
        query_f32 = group_args[0].astype(jnp.float32)
        key_f32 = group_args[1].astype(jnp.float32)
        value_f32 = group_args[2].astype(jnp.float32)
        grad_f32 = group_args[3].astype(jnp.float32)
        scores = jnp.einsum("rqd,kd->rqk", query_f32, key_f32) * score_scale
        masked = jnp.where(allowed[None], scores, very_negative)
        row_max = jnp.max(masked, axis=2, keepdims=True)
        kept = jnp.where(allowed[None], jnp.exp(masked - row_max), 0.0)
        row_lse = row_max + jnp.log(jnp.sum(kept, axis=2, keepdims=True))
        probs_exact = jnp.where(allowed[None], jnp.exp(scores - row_lse), 0.0)
        probs = lax.optimization_barrier(probs_exact.astype(jnp.bfloat16)).astype(jnp.float32)
        attended = jnp.einsum("rqk,kd->rqd", probs, value_f32).astype(jnp.bfloat16)
        attended_f32 = lax.optimization_barrier(attended).astype(jnp.float32)
        delta_rows = jnp.sum(attended_f32 * grad_f32, axis=2, keepdims=True)
        prob_grad = jnp.einsum("rqd,kd->rqk", grad_f32, value_f32)
        score_grad = lax.optimization_barrier((probs_exact * (prob_grad - delta_rows)).astype(jnp.bfloat16)).astype(jnp.float32)
        query_grad = (jnp.einsum("rqk,kd->rqd", score_grad, key_f32) * score_scale).astype(jnp.bfloat16)
        key_gradient = (jnp.einsum("rqk,rqd->kd", score_grad, query_f32) * score_scale).astype(jnp.bfloat16)
        value_gradient = jnp.einsum("rqk,rqd->kd", probs, grad_f32).astype(jnp.bfloat16)
        return attended, query_grad, key_gradient, value_gradient

    attended, query_grad, key_gradient, value_gradient = lax.map(per_group, (heads_of_queries, heads_of_keys, heads_of_values, gradient_heads))
    attended = attended.transpose(2, 0, 1, 3).reshape(count_of_tokens, QUERY_HEADS * HEAD_SIZE)
    query_grad = query_grad.transpose(2, 0, 1, 3).reshape(count_of_tokens, QUERY_HEADS * HEAD_SIZE)
    key_gradient = key_gradient.transpose(1, 0, 2).reshape(count_of_tokens, KEY_VALUE_HEADS * HEAD_SIZE)
    value_gradient = value_gradient.transpose(1, 0, 2).reshape(count_of_tokens, KEY_VALUE_HEADS * HEAD_SIZE)
    return (attended, query_grad, key_gradient, value_gradient)
```

```python
import functools

import jax
import jax.numpy as jnp
from jax import lax
from jax.experimental import pallas as pl
from jax.experimental.pallas import tpu as pltpu
from jax.sharding import PartitionSpec as P

HEAD_SIZE = 128
TILE = 16
SCALE = HEAD_SIZE ** (-0.5)
VERY_NEGATIVE = -1e30
MESH = pl.DeviceIdType.MESH
F32 = jnp.float32
BF16 = jnp.bfloat16

NN = (((1,), (0,)), ((), ()))
NT = (((1,), (1,)), ((), ()))
TN = (((0,), (0,)), ((), ()))


def dot(a, b, dims):
    return lax.dot_general(a, b, dims, preferred_element_type=F32)


def kernel(
    n,
    doc_ref,
    q_ref,
    k_ref,
    v_ref,
    g_ref,
    att_ref,
    dq_ref,
    dk_ref,
    dv_ref,
    kv,
    qs,
    gs,
    gt,
    s_buf,
    dp_buf,
    m_buf,
    l_buf,
    o_buf,
    dq_buf,
    acc,
    outb,
    inb,
    up_send,
    up_recv,
    down_send,
    down_recv,
):
    me = lax.axis_index("seq")
    rows, width = q_ref.shape
    heads = k_ref.shape[1] // HEAD_SIZE
    rep = width // k_ref.shape[1]
    stacked = rep * rows
    last = n - 1
    above, below = lax.rem(me + 1, n), lax.rem(me + n - 1, n)

    def up(b, h):
        return pltpu.make_async_remote_copy(
            src_ref=kv.at[b, h],
            dst_ref=kv.at[b, h],
            send_sem=up_send.at[b, h],
            recv_sem=up_recv.at[b, h],
            device_id={"seq": above},
            device_id_type=MESH,
        )

    def down(b, h, kind):
        return pltpu.make_async_remote_copy(
            src_ref=outb.at[b, h, kind],
            dst_ref=inb.at[b, h, kind],
            send_sem=down_send.at[b, h, kind],
            recv_sem=down_recv.at[b, h, kind],
            device_id={"seq": below},
            device_id_type=MESH,
        )

    barrier = pltpu.get_barrier_semaphore()

    @pl.when(me < last)
    def _():
        pl.semaphore_signal(barrier, inc=1, device_id={"seq": above}, device_id_type=MESH)

    @pl.when(me > 0)
    def _():
        pl.semaphore_signal(barrier, inc=1, device_id={"seq": below}, device_id_type=MESH)

    for h in range(heads):
        kv[me, h, 0] = k_ref[:, h * HEAD_SIZE : (h + 1) * HEAD_SIZE]
        kv[me, h, 1] = v_ref[:, h * HEAD_SIZE : (h + 1) * HEAD_SIZE]

    inner = (me > 0) & (me < last)

    @pl.when(inner)
    def _():
        pl.semaphore_wait(barrier, 2)

    @pl.when(jnp.logical_not(inner))
    def _():
        pl.semaphore_wait(barrier, 1)

    @pl.when(me < last)
    def _():
        for h in range(heads):
            up(me, h).start()

    for h in range(heads):
        for r in range(rep):
            col = (h * rep + r) * HEAD_SIZE
            qs[h, r * rows : (r + 1) * rows] = q_ref[:, col : col + HEAD_SIZE]
            g_part = g_ref[:, col : col + HEAD_SIZE]
            gs[h, r * rows : (r + 1) * rows] = g_part
            gt[h, :, r * rows : (r + 1) * rows] = g_part.astype(F32).T

    column = lax.broadcasted_iota(jnp.int32, (1, stacked), 1)
    query_pos = me * rows + lax.rem(column, rows)
    first = jnp.zeros((1, stacked), jnp.int32)
    begin = jnp.int32(0)
    for d in range(doc_ref.shape[0]):
        first = jnp.where(begin <= query_pos, begin, first)
        begin = begin + doc_ref[d] * TILE
    key_row = lax.broadcasted_iota(jnp.int32, (rows, stacked), 0)

    for h in range(heads):
        m_buf[h] = jnp.full((1, stacked), VERY_NEGATIVE, F32)
        l_buf[h] = jnp.zeros((1, stacked), F32)
        o_buf[h] = jnp.zeros((HEAD_SIZE, stacked), F32)
        dq_buf[h] = jnp.zeros((HEAD_SIZE, stacked), F32)

    def arrive(t, carry):
        b = me - t

        @pl.when(t > 0)
        def _():
            for h in range(heads):
                up(b, h).wait_recv()

                @pl.when(me < last)
                def _():
                    up(b, h).start()

        key_pos = b * rows + key_row
        allowed = (key_pos >= first) & (key_pos <= query_pos)
        for h in range(heads):
            scores = dot(kv[b, h, 0], qs[h], NT) * SCALE
            scores = jnp.where(allowed, scores, VERY_NEGATIVE)
            s_buf[b, h] = scores
            old = m_buf[h]
            new = jnp.maximum(old, jnp.max(scores, axis=0, keepdims=True))
            total = jnp.sum(jnp.exp(scores - new), axis=0, keepdims=True)
            l_buf[h] = l_buf[h] * jnp.exp(old - new) + total
            m_buf[h] = new
            dp_buf[b, h] = dot(kv[b, h, 1], gs[h], NT)
        return carry

    lax.fori_loop(0, me + 1, arrive, 0)

    def emit(b, h, kind, part):
        goes = (me == last) & (b < me)

        @pl.when(goes)
        def _():
            outb[b, h, kind] = part.astype(outb.dtype)
            down(b, h, kind).start()

        @pl.when(jnp.logical_not(goes))
        def _():
            acc[b, h, kind] = part

    for h in range(heads):
        m_buf[h] = m_buf[h] + jnp.log(l_buf[h])

    def value_part(b, carry):
        for h in range(heads):
            probs = jnp.exp(s_buf[b, h] - m_buf[h])
            s_buf[b, h] = probs
            probs_bf = probs.astype(BF16)
            emit(b, h, 1, dot(probs_bf, gs[h], NN))
            o_buf[h] += dot(kv[b, h, 1], probs_bf, TN)
        return carry

    lax.fori_loop(0, me + 1, value_part, 0)

    for h in range(heads):
        rounded = o_buf[h].astype(BF16).astype(F32)
        l_buf[h] = jnp.sum(rounded * gt[h], axis=0, keepdims=True)

    def key_part(b, carry):
        for h in range(heads):
            score_grad = (s_buf[b, h] * (dp_buf[b, h] - l_buf[h])).astype(BF16)
            emit(b, h, 0, dot(score_grad, qs[h], NN))
            dq_buf[h] += dot(kv[b, h, 0], score_grad, TN)
        return carry

    lax.fori_loop(0, me + 1, key_part, 0)

    for h in range(heads):
        for r in range(rep):
            col = (h * rep + r) * HEAD_SIZE
            part = o_buf[h, :, r * rows : (r + 1) * rows]
            att_ref[:, col : col + HEAD_SIZE] = part.T.astype(BF16)
            part = dq_buf[h, :, r * rows : (r + 1) * rows] * SCALE
            dq_ref[:, col : col + HEAD_SIZE] = part.T.astype(BF16)

    def finish(h, kind, total):
        cols = slice(h * HEAD_SIZE, (h + 1) * HEAD_SIZE)
        if kind == 1:
            dv_ref[:, cols] = total.astype(BF16)
        else:
            dk_ref[:, cols] = (total * SCALE).astype(BF16)

    @pl.when(me < last)
    def _():
        for kind in (1, 0):

            def pass_on(b, carry):
                for h in range(heads):
                    down(b, h, kind).wait_recv()
                    outb[b, h, kind] = (
                        acc[b, h, kind] + inb[b, h, kind].astype(F32)
                    ).astype(outb.dtype)
                    down(b, h, kind).start()
                return carry

            lax.fori_loop(0, me, pass_on, 0)
            for h in range(heads):
                down(me, h, kind).wait_recv()
                finish(h, kind, acc[me, h, kind] + inb[me, h, kind].astype(F32))

    @pl.when(me == last)
    def _():
        for h in range(heads):
            for kind in (1, 0):
                finish(h, kind, acc[me, h, kind])

    @pl.when(me < last)
    def _():
        def sent(b, carry):
            for h in range(heads):
                up(b, h).wait_send()
            return carry

        lax.fori_loop(0, me + 1, sent, 0)

    def returned(b, carry):
        for h in range(heads):
            for kind in (1, 0):
                down(b, h, kind).wait_send()
        return carry

    lax.fori_loop(0, me, returned, 0)


def per_device(queries, keys, values, output_gradient, doc_tiles):
    n = lax.axis_size("seq")
    rows, width = queries.shape
    heads = keys.shape[1] // HEAD_SIZE
    stacked = rows * width // keys.shape[1]
    travel = BF16 if n <= 8 else F32
    vmem = pl.BlockSpec(memory_space=pltpu.VMEM)
    block = (n, heads, 2, rows, HEAD_SIZE)
    return pl.pallas_call(
        functools.partial(kernel, n),
        out_shape=(
            jax.ShapeDtypeStruct(queries.shape, BF16),
            jax.ShapeDtypeStruct(queries.shape, BF16),
            jax.ShapeDtypeStruct(keys.shape, BF16),
            jax.ShapeDtypeStruct(keys.shape, BF16),
        ),
        in_specs=[pl.BlockSpec(memory_space=pltpu.SMEM)] + [vmem] * 4,
        out_specs=(vmem,) * 4,
        scratch_shapes=[
            pltpu.VMEM(block, BF16),
            pltpu.VMEM((heads, stacked, HEAD_SIZE), BF16),
            pltpu.VMEM((heads, stacked, HEAD_SIZE), BF16),
            pltpu.VMEM((heads, HEAD_SIZE, stacked), F32),
            pltpu.VMEM((n, heads, rows, stacked), F32),
            pltpu.VMEM((n, heads, rows, stacked), F32),
            pltpu.VMEM((heads, 1, stacked), F32),
            pltpu.VMEM((heads, 1, stacked), F32),
            pltpu.VMEM((heads, HEAD_SIZE, stacked), F32),
            pltpu.VMEM((heads, HEAD_SIZE, stacked), F32),
            pltpu.VMEM(block, F32),
            pltpu.VMEM(block, travel),
            pltpu.VMEM(block, travel),
            pltpu.SemaphoreType.DMA((n, heads)),
            pltpu.SemaphoreType.DMA((n, heads)),
            pltpu.SemaphoreType.DMA((n, heads, 2)),
            pltpu.SemaphoreType.DMA((n, heads, 2)),
        ],
        compiler_params=pltpu.CompilerParams(
            collective_id=0, has_side_effects=True, vmem_limit_bytes=50 * 1024 * 1024
        ),
        cost_estimate=pl.CostEstimate(
            flops=12 * n * heads * rows * stacked * HEAD_SIZE,
            bytes_accessed=8 * rows * width,
            transcendentals=2 * n * heads * rows * stacked,
        ),
    )(doc_tiles, queries, keys, values, output_gradient)


def solution(mesh):
    rows = P(("grp", "seq"), "sub")
    return jax.shard_map(
        per_device,
        mesh=mesh,
        in_specs=(rows, rows, rows, rows, P("grp")),
        out_specs=(rows, rows, rows, rows),
        check_vma=False,
    )
```

```python
import functools

import jax
import jax.numpy as jnp
from jax import lax
from jax.experimental import pallas as pl
from jax.experimental.pallas import tpu as pltpu
from jax.sharding import PartitionSpec as P

HEAD_SIZE = 128
TILE = 16
SCALE = HEAD_SIZE ** (-0.5)
VERY_NEGATIVE = -1e30
VMEM_BYTES = 64 * 1024 * 1024
MESH = pl.DeviceIdType.MESH
F32 = jnp.float32
BF16 = jnp.bfloat16

NN = (((1,), (0,)), ((), ()))
NT = (((1,), (1,)), ((), ()))
TN = (((0,), (0,)), ((), ()))


def dot(a, b, dims):
    return lax.dot_general(a, b, dims, preferred_element_type=F32)


def loop(start, stop, body):
    if isinstance(start, int) and isinstance(stop, int):
        for x in range(start, stop):
            body(x)
    else:

        def step(x, carry):
            body(x)
            return carry

        lax.fori_loop(start, stop, step, 0)


def kernel(
    n,
    doc_hbm,
    q_ref,
    k_ref,
    v_ref,
    g_ref,
    att_hbm,
    dq_hbm,
    dk_hbm,
    dv_hbm,
    att_ref,
    dq_ref,
    dk_ref,
    dv_ref,
    doc_ref,
    kv,
    qs,
    gs,
    gt,
    s_buf,
    dp_buf,
    m_buf,
    l_buf,
    o_buf,
    dq_buf,
    acc,
    outb,
    inb,
    doc_sem,
    kv_sem,
    q_sem,
    up_send,
    up_recv,
    down_send,
    down_recv,
    out_sem,
):
    me = lax.axis_index("seq")
    rows, width = q_ref.shape
    heads = k_ref.shape[1] // HEAD_SIZE
    rep = width // k_ref.shape[1]
    stacked = rep * rows

    results = [
        pltpu.make_async_copy(src, dst, out_sem.at[i])
        for i, (src, dst) in enumerate(
            ((att_ref, att_hbm), (dq_ref, dq_hbm), (dk_ref, dk_hbm), (dv_ref, dv_hbm))
        )
    ]

    def head_cols(h):
        return slice(h * HEAD_SIZE, (h + 1) * HEAD_SIZE)

    def own_kv(h, kind):
        src = (k_ref, v_ref)[kind].at[:, head_cols(h)]
        return pltpu.make_async_copy(src, kv.at[me, h, kind], kv_sem.at[h, kind])

    def own_rows(h, r, kind):
        src = (q_ref, g_ref)[kind].at[:, head_cols(h * rep + r)]
        dst = (qs, gs)[kind].at[h, pl.ds(r * rows, rows)]
        return pltpu.make_async_copy(src, dst, q_sem.at[h, r, kind])

    barrier = pltpu.get_barrier_semaphore()
    for d in range(1, n):
        other = lax.rem(me + d, n)
        pl.semaphore_signal(barrier, inc=1, device_id={"seq": other}, device_id_type=MESH)

    pairs = [(h, kind) for h in range(heads) for kind in range(2)]
    for h, kind in pairs:
        own_kv(h, kind).start()
    doc_copy = pltpu.make_async_copy(doc_hbm, doc_ref, doc_sem)
    doc_copy.start()
    for h, kind in pairs:
        for r in range(rep):
            own_rows(h, r, kind).start()

    for h, kind in pairs:
        own_kv(h, kind).wait()
    pl.semaphore_wait(barrier, n - 1)

    def run(me):
        def up(src, target, h):
            return pltpu.make_async_remote_copy(
                src_ref=kv.at[src, h],
                dst_ref=kv.at[src, h],
                send_sem=up_send.at[target, h],
                recv_sem=up_recv.at[src, h],
                device_id={"seq": target},
                device_id_type=MESH,
            )

        def down(src, target, h, kind):
            return pltpu.make_async_remote_copy(
                src_ref=outb.at[target, h, kind],
                dst_ref=inb.at[src, h, kind],
                send_sem=down_send.at[target, h, kind],
                recv_sem=down_recv.at[src, h, kind],
                device_id={"seq": target},
                device_id_type=MESH,
            )

        for h in range(heads):
            loop(0, n - 1 - me, lambda x: up(me, n - 1 - x, h).start())

        doc_copy.wait()
        column = lax.broadcasted_iota(jnp.int32, (1, stacked), 1)
        query_pos = me * rows + lax.rem(column, rows)
        first = jnp.zeros((1, stacked), jnp.int32)
        begin = jnp.int32(0)
        for d in range(doc_ref.shape[0]):
            first = jnp.where(begin <= query_pos, begin, first)
            begin = begin + doc_ref[d] * TILE
        key_row = lax.broadcasted_iota(jnp.int32, (rows, stacked), 0)

        def scores_of(b, h):
            key_pos = b * rows + key_row
            allowed = (key_pos >= first) & (key_pos <= query_pos)
            scores = dot(kv[b, h, 0], qs[h], NT) * SCALE
            scores = jnp.where(allowed, scores, VERY_NEGATIVE)
            s_buf[b, h] = scores
            dp_buf[b, h] = dot(kv[b, h, 1], gs[h], NT)
            return scores, jnp.max(scores, axis=0, keepdims=True)

        for h in range(heads):
            for r in range(rep):
                for kind in range(2):
                    own_rows(h, r, kind).wait()
            scores, top = scores_of(me, h)
            m_buf[h] = top
            l_buf[h] = jnp.sum(jnp.exp(scores - top), axis=0, keepdims=True)
            gt[h] = gs[h].astype(F32).T
            o_buf[h] = jnp.zeros((HEAD_SIZE, stacked), F32)
            dq_buf[h] = jnp.zeros((HEAD_SIZE, stacked), F32)

        def emit(b, h, kind, part):
            outb[b, h, kind] = part.astype(BF16)
            down(me, b, h, kind).start()

        for h in range(heads):

            def arrive(t):
                b = me - t
                up(b, me, h).wait_recv()
                scores, top = scores_of(b, h)
                old = m_buf[h]
                new = jnp.maximum(old, top)
                total = jnp.sum(jnp.exp(scores - new), axis=0, keepdims=True)
                l_buf[h] = l_buf[h] * jnp.exp(old - new) + total
                m_buf[h] = new

            loop(1, me + 1, arrive)
            lse = m_buf[h] + jnp.log(l_buf[h])
            m_buf[h] = lse

            def value_part(b):
                probs = jnp.exp(s_buf[b, h] - m_buf[h])
                s_buf[b, h] = probs
                probs_bf = probs.astype(BF16)
                o_buf[h] += dot(kv[b, h, 1], probs_bf, TN)
                return dot(probs_bf, gs[h], NN)

            loop(0, me, lambda b: emit(b, h, 1, value_part(b)))
            acc[h, 1] = value_part(me)

            rounded = o_buf[h].astype(BF16).astype(F32)
            l_buf[h] = jnp.sum(rounded * gt[h], axis=0, keepdims=True)

            def key_part(b):
                score_grad = (s_buf[b, h] * (dp_buf[b, h] - l_buf[h])).astype(BF16)
                dq_buf[h] += dot(kv[b, h, 0], score_grad, TN)
                return dot(score_grad, qs[h], NN)

            loop(0, me, lambda b: emit(b, h, 0, key_part(b)))
            acc[h, 0] = key_part(me)

        for h in range(heads):
            for r in range(rep):
                part = o_buf[h, :, r * rows : (r + 1) * rows]
                att_ref[:, head_cols(h * rep + r)] = part.T.astype(BF16)
                part = dq_buf[h, :, r * rows : (r + 1) * rows] * SCALE
                dq_ref[:, head_cols(h * rep + r)] = part.T.astype(BF16)
        results[0].start()
        results[1].start()

        for h in range(heads):
            for kind in (1, 0):

                def add(x):
                    src = n - 1 - x
                    down(src, me, h, kind).wait_recv()
                    acc[h, kind] += inb[src, h, kind].astype(F32)

                loop(0, n - 1 - me, add)
                if kind == 1:
                    dv_ref[:, head_cols(h)] = acc[h, 1].astype(BF16)
                else:
                    dk_ref[:, head_cols(h)] = (acc[h, 0] * SCALE).astype(BF16)

        results[2].start()
        results[3].start()

        for h in range(heads):
            loop(0, n - 1 - me, lambda x: up(me, n - 1 - x, h).wait_send())
            for kind in (1, 0):
                loop(0, me, lambda b: down(me, b, h, kind).wait_send())
        for copy in results:
            copy.wait()

    if n <= 4:
        for i in range(n):
            pl.when(me == i)(functools.partial(run, i))
    else:
        run(me)


def write_out(*refs):
    count = len(refs) // 2
    sems = refs[-1]
    copies = [
        pltpu.make_async_copy(refs[i], refs[count + i], sems.at[i]) for i in range(count)
    ]
    for copy in copies:
        copy.start()
    for copy in copies:
        copy.wait()


def per_device(queries, keys, values, output_gradient, doc_tiles):
    n = lax.axis_size("seq")
    rows, width = queries.shape
    heads = keys.shape[1] // HEAD_SIZE
    rep = width // keys.shape[1]
    stacked = rows * rep
    hbm = pl.BlockSpec(memory_space=pltpu.HBM)
    block = (n, heads, 2, rows, HEAD_SIZE)
    shapes = (
        jax.ShapeDtypeStruct(queries.shape, BF16),
        jax.ShapeDtypeStruct(queries.shape, BF16),
        jax.ShapeDtypeStruct(keys.shape, BF16),
        jax.ShapeDtypeStruct(keys.shape, BF16),
    )
    dma = pltpu.SemaphoreType.DMA
    results = pl.pallas_call(
        functools.partial(kernel, n),
        out_shape=shapes,
        in_specs=[hbm] * 5,
        out_specs=(hbm,) * 4,
        scratch_shapes=[
            pltpu.VMEM(queries.shape, BF16),
            pltpu.VMEM(queries.shape, BF16),
            pltpu.VMEM(keys.shape, BF16),
            pltpu.VMEM(keys.shape, BF16),
            pltpu.SMEM(doc_tiles.shape, jnp.int32),
            pltpu.VMEM(block, BF16),
            pltpu.VMEM((heads, stacked, HEAD_SIZE), BF16),
            pltpu.VMEM((heads, stacked, HEAD_SIZE), BF16),
            pltpu.VMEM((heads, HEAD_SIZE, stacked), F32),
            pltpu.VMEM((n, heads, rows, stacked), F32),
            pltpu.VMEM((n, heads, rows, stacked), F32),
            pltpu.VMEM((heads, 1, stacked), F32),
            pltpu.VMEM((heads, 1, stacked), F32),
            pltpu.VMEM((heads, HEAD_SIZE, stacked), F32),
            pltpu.VMEM((heads, HEAD_SIZE, stacked), F32),
            pltpu.VMEM((heads, 2, rows, HEAD_SIZE), F32),
            pltpu.VMEM(block, BF16),
            pltpu.VMEM(block, BF16),
            dma,
            dma((heads, 2)),
            dma((heads, rep, 2)),
            dma((n, heads)),
            dma((n, heads)),
            dma((n, heads, 2)),
            dma((n, heads, 2)),
            dma((4,)),
        ],
        compiler_params=pltpu.CompilerParams(
            collective_id=0, has_side_effects=True, vmem_limit_bytes=VMEM_BYTES
        ),
        cost_estimate=pl.CostEstimate(
            flops=12 * n * heads * rows * stacked * HEAD_SIZE,
            bytes_accessed=8 * rows * width,
            transcendentals=2 * n * heads * rows * stacked,
        ),
    )(doc_tiles, queries, keys, values, output_gradient)
    return pl.pallas_call(
        write_out,
        out_shape=shapes,
        in_specs=[hbm] * 4,
        out_specs=(hbm,) * 4,
        scratch_shapes=[dma((4,))],
        compiler_params=pltpu.CompilerParams(vmem_limit_bytes=VMEM_BYTES),
    )(*results)


def solution(mesh):
    rows = P(("grp", "seq"), "sub")
    return jax.shard_map(
        per_device,
        mesh=mesh,
        in_specs=(rows, rows, rows, rows, P("grp")),
        out_specs=(rows, rows, rows, rows),
        check_vma=False,
    )
```

```python
import functools

import jax
import jax.numpy as jnp
from jax import lax
from jax.experimental import pallas as pl
from jax.experimental.pallas import tpu as pltpu
from jax.sharding import PartitionSpec as P

HEAD_SIZE = 128
TILE = 16
SCALE = HEAD_SIZE ** (-0.5)
VERY_NEGATIVE = -1e30
VMEM_BYTES = 64 * 1024 * 1024
MESH = pl.DeviceIdType.MESH
F32 = jnp.float32
BF16 = jnp.bfloat16

NN = (((1,), (0,)), ((), ()))
NT = (((1,), (1,)), ((), ()))
TN = (((0,), (0,)), ((), ()))


def dot(a, b, dims):
    return lax.dot_general(a, b, dims, preferred_element_type=F32)


def loop(start, stop, body):
    if isinstance(start, int) and isinstance(stop, int):
        for x in range(start, stop):
            body(x)
    else:

        def step(x, carry):
            body(x)
            return carry

        lax.fori_loop(start, stop, step, 0)


def kernel(
    n,
    doc_hbm,
    q_ref,
    k_ref,
    v_ref,
    g_ref,
    att_hbm,
    dq_hbm,
    dk_hbm,
    dv_hbm,
    att_ref,
    dq_ref,
    dk_ref,
    dv_ref,
    doc_ref,
    kv,
    qs,
    gs,
    gt,
    s_buf,
    dp_buf,
    m_buf,
    l_buf,
    o_buf,
    dq_buf,
    acc,
    outb,
    inb,
    doc_sem,
    kv_sem,
    q_sem,
    up_send,
    up_recv,
    down_send,
    down_recv,
    out_sem,
):
    me = lax.axis_index("seq")
    rows, width = q_ref.shape
    heads = k_ref.shape[1] // HEAD_SIZE
    rep = width // k_ref.shape[1]
    stacked = rep * rows

    results = [
        pltpu.make_async_copy(src, dst, out_sem.at[i])
        for i, (src, dst) in enumerate(
            ((att_ref, att_hbm), (dq_ref, dq_hbm), (dk_ref, dk_hbm), (dv_ref, dv_hbm))
        )
    ]

    def head_cols(h):
        return slice(h * HEAD_SIZE, (h + 1) * HEAD_SIZE)

    def own_kv(h, kind):
        src = (k_ref, v_ref)[kind].at[:, head_cols(h)]
        return pltpu.make_async_copy(src, kv.at[me, h, kind], kv_sem.at[h, kind])

    def own_rows(h, r, kind):
        src = (q_ref, g_ref)[kind].at[:, head_cols(h * rep + r)]
        dst = (qs, gs)[kind].at[h, pl.ds(r * rows, rows)]
        return pltpu.make_async_copy(src, dst, q_sem.at[h, r, kind])

    barrier = pltpu.get_barrier_semaphore()
    for d in range(1, n):
        other = lax.rem(me + d, n)
        pl.semaphore_signal(barrier, inc=1, device_id={"seq": other}, device_id_type=MESH)

    pairs = [(h, kind) for h in range(heads) for kind in range(2)]
    for h, kind in pairs:
        own_kv(h, kind).start()
    doc_copy = pltpu.make_async_copy(doc_hbm, doc_ref, doc_sem)
    doc_copy.start()
    for h, kind in pairs:
        for r in range(rep):
            own_rows(h, r, kind).start()

    for h, kind in pairs:
        own_kv(h, kind).wait()
    pl.semaphore_wait(barrier, n - 1)

    def run(me):
        def up(src, target, h):
            return pltpu.make_async_remote_copy(
                src_ref=kv.at[src, h],
                dst_ref=kv.at[src, h],
                send_sem=up_send.at[target, h],
                recv_sem=up_recv.at[src, h],
                device_id={"seq": target},
                device_id_type=MESH,
            )

        def down(src, target, h, kind):
            return pltpu.make_async_remote_copy(
                src_ref=outb.at[target, h, kind],
                dst_ref=inb.at[src, h, kind],
                send_sem=down_send.at[target, h, kind],
                recv_sem=down_recv.at[src, h, kind],
                device_id={"seq": target},
                device_id_type=MESH,
            )

        for h in range(heads):
            loop(0, n - 1 - me, lambda x: up(me, n - 1 - x, h).start())

        doc_copy.wait()
        column = lax.broadcasted_iota(jnp.int32, (1, stacked), 1)
        query_pos = me * rows + lax.rem(column, rows)
        first = jnp.zeros((1, stacked), jnp.int32)
        begin = jnp.int32(0)
        for d in range(doc_ref.shape[0]):
            first = jnp.where(begin <= query_pos, begin, first)
            begin = begin + doc_ref[d] * TILE
        key_row = lax.broadcasted_iota(jnp.int32, (rows, stacked), 0)

        def scores_of(b, h):
            key_pos = b * rows + key_row
            allowed = (key_pos >= first) & (key_pos <= query_pos)
            scores = dot(kv[b, h, 0], qs[h], NT) * SCALE
            scores = jnp.where(allowed, scores, VERY_NEGATIVE)
            s_buf[b, h] = scores
            dp_buf[b, h] = dot(kv[b, h, 1], gs[h], NT)
            return scores, jnp.max(scores, axis=0, keepdims=True)

        for h in range(heads):
            for r in range(rep):
                for kind in range(2):
                    own_rows(h, r, kind).wait()
            scores, top = scores_of(me, h)
            m_buf[h] = top
            l_buf[h] = jnp.sum(jnp.exp(scores - top), axis=0, keepdims=True)
            gt[h] = gs[h].astype(F32).T
            o_buf[h] = jnp.zeros((HEAD_SIZE, stacked), F32)
            dq_buf[h] = jnp.zeros((HEAD_SIZE, stacked), F32)

        def emit(b, h, kind, part):
            outb[b, h, kind] = part.astype(BF16)
            down(me, b, h, kind).start()

        for h in range(heads):

            def arrive(t):
                b = me - t
                up(b, me, h).wait_recv()
                scores, top = scores_of(b, h)
                old = m_buf[h]
                new = jnp.maximum(old, top)
                total = jnp.sum(jnp.exp(scores - new), axis=0, keepdims=True)
                l_buf[h] = l_buf[h] * jnp.exp(old - new) + total
                m_buf[h] = new

            loop(1, me + 1, arrive)
            lse = m_buf[h] + jnp.log(l_buf[h])
            m_buf[h] = lse

            def value_part(b):
                probs = jnp.exp(s_buf[b, h] - m_buf[h])
                s_buf[b, h] = probs
                probs_bf = probs.astype(BF16)
                o_buf[h] += dot(kv[b, h, 1], probs_bf, TN)
                return dot(probs_bf, gs[h], NN)

            loop(0, me, lambda b: emit(b, h, 1, value_part(b)))
            acc[h, 1] = value_part(me)

            rounded = o_buf[h].astype(BF16).astype(F32)
            l_buf[h] = jnp.sum(rounded * gt[h], axis=0, keepdims=True)

            def key_part(b):
                score_grad = (s_buf[b, h] * (dp_buf[b, h] - l_buf[h])).astype(BF16)
                dq_buf[h] += dot(kv[b, h, 0], score_grad, TN)
                return dot(score_grad, qs[h], NN)

            loop(0, me, lambda b: emit(b, h, 0, key_part(b)))
            acc[h, 0] = key_part(me)

        for h in range(heads):
            for r in range(rep):
                part = o_buf[h, :, r * rows : (r + 1) * rows]
                att_ref[:, head_cols(h * rep + r)] = part.T.astype(BF16)
                part = dq_buf[h, :, r * rows : (r + 1) * rows] * SCALE
                dq_ref[:, head_cols(h * rep + r)] = part.T.astype(BF16)
        results[0].start()
        results[1].start()

        for h in range(heads):
            for kind in (1, 0):

                def add(x):
                    src = n - 1 - x
                    down(src, me, h, kind).wait_recv()
                    acc[h, kind] += inb[src, h, kind].astype(F32)

                loop(0, n - 1 - me, add)
                if kind == 1:
                    dv_ref[:, head_cols(h)] = acc[h, 1].astype(BF16)
                else:
                    dk_ref[:, head_cols(h)] = (acc[h, 0] * SCALE).astype(BF16)

        results[2].start()
        results[3].start()

        for h in range(heads):
            loop(0, n - 1 - me, lambda x: up(me, n - 1 - x, h).wait_send())
            for kind in (1, 0):
                loop(0, me, lambda b: down(me, b, h, kind).wait_send())
        for copy in results:
            copy.wait()

    if n <= 4:
        for i in range(n):
            pl.when(me == i)(functools.partial(run, i))
    else:
        run(me)


def write_out(*refs):
    count = 4
    sources, targets, held = refs[:count], refs[count : 2 * count], refs[2 * count : 3 * count]
    sems = refs[3 * count]
    arriving = [
        pltpu.make_async_copy(sources[i], held[i], sems.at[0, i]) for i in range(count)
    ]
    leaving = [pltpu.make_async_copy(held[i], targets[i], sems.at[1, i]) for i in range(count)]
    for copy in arriving:
        copy.start()
    for i in range(count):
        arriving[i].wait()
        leaving[i].start()
    for copy in leaving:
        copy.wait()


def per_device(queries, keys, values, output_gradient, doc_tiles):
    n = lax.axis_size("seq")
    rows, width = queries.shape
    heads = keys.shape[1] // HEAD_SIZE
    rep = width // keys.shape[1]
    stacked = rows * rep
    hbm = pl.BlockSpec(memory_space=pltpu.HBM)
    block = (n, heads, 2, rows, HEAD_SIZE)
    shapes = (
        jax.ShapeDtypeStruct(queries.shape, BF16),
        jax.ShapeDtypeStruct(queries.shape, BF16),
        jax.ShapeDtypeStruct(keys.shape, BF16),
        jax.ShapeDtypeStruct(keys.shape, BF16),
    )
    dma = pltpu.SemaphoreType.DMA
    results = pl.pallas_call(
        functools.partial(kernel, n),
        out_shape=shapes,
        in_specs=[hbm] * 5,
        out_specs=(hbm,) * 4,
        scratch_shapes=[
            pltpu.VMEM(queries.shape, BF16),
            pltpu.VMEM(queries.shape, BF16),
            pltpu.VMEM(keys.shape, BF16),
            pltpu.VMEM(keys.shape, BF16),
            pltpu.SMEM(doc_tiles.shape, jnp.int32),
            pltpu.VMEM(block, BF16),
            pltpu.VMEM((heads, stacked, HEAD_SIZE), BF16),
            pltpu.VMEM((heads, stacked, HEAD_SIZE), BF16),
            pltpu.VMEM((heads, HEAD_SIZE, stacked), F32),
            pltpu.VMEM((n, heads, rows, stacked), F32),
            pltpu.VMEM((n, heads, rows, stacked), F32),
            pltpu.VMEM((heads, 1, stacked), F32),
            pltpu.VMEM((heads, 1, stacked), F32),
            pltpu.VMEM((heads, HEAD_SIZE, stacked), F32),
            pltpu.VMEM((heads, HEAD_SIZE, stacked), F32),
            pltpu.VMEM((heads, 2, rows, HEAD_SIZE), F32),
            pltpu.VMEM(block, BF16),
            pltpu.VMEM(block, BF16),
            dma,
            dma((heads, 2)),
            dma((heads, rep, 2)),
            dma((n, heads)),
            dma((n, heads)),
            dma((n, heads, 2)),
            dma((n, heads, 2)),
            dma((4,)),
        ],
        compiler_params=pltpu.CompilerParams(
            collective_id=0, has_side_effects=True, vmem_limit_bytes=VMEM_BYTES
        ),
        cost_estimate=pl.CostEstimate(
            flops=12 * n * heads * rows * stacked * HEAD_SIZE,
            bytes_accessed=8 * rows * width,
            transcendentals=2 * n * heads * rows * stacked,
        ),
    )(doc_tiles, queries, keys, values, output_gradient)
    return pl.pallas_call(
        write_out,
        out_shape=shapes,
        in_specs=[hbm] * 4,
        out_specs=(hbm,) * 4,
        scratch_shapes=[pltpu.VMEM(shape.shape, BF16) for shape in shapes] + [dma((2, 4))],
        compiler_params=pltpu.CompilerParams(vmem_limit_bytes=VMEM_BYTES),
    )(*results)


def solution(mesh):
    rows = P(("grp", "seq"), "sub")
    return jax.shard_map(
        per_device,
        mesh=mesh,
        in_specs=(rows, rows, rows, rows, P("grp")),
        out_specs=(rows, rows, rows, rows),
        check_vma=False,
    )
```

```python
import functools

import jax
import jax.numpy as jnp
from jax import lax
from jax.experimental import pallas as pl
from jax.experimental.pallas import tpu as pltpu
from jax.sharding import PartitionSpec as P

HEAD_SIZE = 128
TILE = 16
SCALE = HEAD_SIZE ** (-0.5)
VERY_NEGATIVE = -1e30
VMEM_BYTES = 64 * 1024 * 1024
MESH = pl.DeviceIdType.MESH
F32 = jnp.float32
BF16 = jnp.bfloat16

NN = (((1,), (0,)), ((), ()))
NT = (((1,), (1,)), ((), ()))
TN = (((0,), (0,)), ((), ()))


def dot(a, b, dims):
    return lax.dot_general(a, b, dims, preferred_element_type=F32)


def loop(start, stop, body):
    if isinstance(start, int) and isinstance(stop, int):
        for x in range(start, stop):
            body(x)
    else:

        def step(x, carry):
            body(x)
            return carry

        lax.fori_loop(start, stop, step, 0)


def kernel(
    n,
    doc_hbm,
    q_ref,
    k_ref,
    v_ref,
    g_ref,
    att_hbm,
    dq_hbm,
    dk_hbm,
    dv_hbm,
    att_ref,
    dq_ref,
    dk_ref,
    dv_ref,
    doc_ref,
    kv,
    qs,
    gs,
    gt,
    s_buf,
    dp_buf,
    m_buf,
    l_buf,
    o_buf,
    dq_buf,
    acc,
    outb,
    inb,
    doc_sem,
    kv_sem,
    q_sem,
    up_send,
    up_recv,
    down_send,
    down_recv,
    out_sem,
):
    me = lax.axis_index("seq")
    rows, width = q_ref.shape
    heads = k_ref.shape[1] // HEAD_SIZE
    rep = width // k_ref.shape[1]
    stacked = rep * rows

    results = [
        pltpu.make_async_copy(src, dst, out_sem.at[i])
        for i, (src, dst) in enumerate(
            ((att_ref, att_hbm), (dq_ref, dq_hbm), (dk_ref, dk_hbm), (dv_ref, dv_hbm))
        )
    ]

    def head_cols(h):
        return slice(h * HEAD_SIZE, (h + 1) * HEAD_SIZE)

    def own_kv(h, kind):
        src = (k_ref, v_ref)[kind].at[:, head_cols(h)]
        return pltpu.make_async_copy(src, kv.at[me, h, kind], kv_sem.at[h, kind])

    def own_rows(h, r, kind):
        src = (q_ref, g_ref)[kind].at[:, head_cols(h * rep + r)]
        dst = (qs, gs)[kind].at[h, pl.ds(r * rows, rows)]
        return pltpu.make_async_copy(src, dst, q_sem.at[h, r, kind])

    barrier = pltpu.get_barrier_semaphore()
    for d in range(1, n):
        other = lax.rem(me + d, n)
        pl.semaphore_signal(barrier, inc=1, device_id={"seq": other}, device_id_type=MESH)

    pairs = [(h, kind) for h in range(heads) for kind in range(2)]
    for h, kind in pairs:
        own_kv(h, kind).start()
    doc_copy = pltpu.make_async_copy(doc_hbm, doc_ref, doc_sem)
    doc_copy.start()
    for h, kind in pairs:
        for r in range(rep):
            own_rows(h, r, kind).start()

    for h, kind in pairs:
        own_kv(h, kind).wait()
    pl.semaphore_wait(barrier, n - 1)

    def run(me):
        def up(src, target, h):
            return pltpu.make_async_remote_copy(
                src_ref=kv.at[src, h],
                dst_ref=kv.at[src, h],
                send_sem=up_send.at[target, h],
                recv_sem=up_recv.at[src, h],
                device_id={"seq": target},
                device_id_type=MESH,
            )

        def down(src, target, h, kind):
            return pltpu.make_async_remote_copy(
                src_ref=outb.at[target, h, kind],
                dst_ref=inb.at[src, h, kind],
                send_sem=down_send.at[target, h, kind],
                recv_sem=down_recv.at[src, h, kind],
                device_id={"seq": target},
                device_id_type=MESH,
            )

        relayed = n == 4
        skip = 1 if relayed and me == 0 else 0

        def forward(h):
            return pltpu.make_async_remote_copy(
                src_ref=kv.at[0, h],
                dst_ref=kv.at[0, h],
                send_sem=up_send.at[0, h],
                recv_sem=up_recv.at[0, h],
                device_id={"seq": 3},
                device_id_type=MESH,
            )

        def relay(h):
            if relayed and me == 2:
                up(0, me, h).wait_recv()
                forward(h).start()

        for h in range(heads):
            loop(skip, n - 1 - me, lambda x: up(me, n - 1 - x, h).start())

        doc_copy.wait()
        column = lax.broadcasted_iota(jnp.int32, (1, stacked), 1)
        query_pos = me * rows + lax.rem(column, rows)
        first = jnp.zeros((1, stacked), jnp.int32)
        begin = jnp.int32(0)
        for d in range(doc_ref.shape[0]):
            first = jnp.where(begin <= query_pos, begin, first)
            begin = begin + doc_ref[d] * TILE
        key_row = lax.broadcasted_iota(jnp.int32, (rows, stacked), 0)

        def scores_of(b, h):
            key_pos = b * rows + key_row
            allowed = (key_pos >= first) & (key_pos <= query_pos)
            scores = dot(kv[b, h, 0], qs[h], NT) * SCALE
            scores = jnp.where(allowed, scores, VERY_NEGATIVE)
            s_buf[b, h] = scores
            dp_buf[b, h] = dot(kv[b, h, 1], gs[h], NT)
            return scores, jnp.max(scores, axis=0, keepdims=True)

        for h in range(heads):
            for r in range(rep):
                for kind in range(2):
                    own_rows(h, r, kind).wait()
            scores, top = scores_of(me, h)
            m_buf[h] = top
            l_buf[h] = jnp.sum(jnp.exp(scores - top), axis=0, keepdims=True)
            gt[h] = gs[h].astype(F32).T
            o_buf[h] = jnp.zeros((HEAD_SIZE, stacked), F32)
            dq_buf[h] = jnp.zeros((HEAD_SIZE, stacked), F32)

        def emit(b, h, kind, part):
            outb[b, h, kind] = part.astype(BF16)
            down(me, b, h, kind).start()

        relay(0)
        for h in range(heads):

            def arrive(t):
                b = me - t
                if not (relayed and me == 2 and b == 0):
                    up(b, me, h).wait_recv()
                scores, top = scores_of(b, h)
                old = m_buf[h]
                new = jnp.maximum(old, top)
                total = jnp.sum(jnp.exp(scores - new), axis=0, keepdims=True)
                l_buf[h] = l_buf[h] * jnp.exp(old - new) + total
                m_buf[h] = new

            loop(1, me + 1, arrive)
            lse = m_buf[h] + jnp.log(l_buf[h])
            m_buf[h] = lse

            def value_part(b):
                probs = jnp.exp(s_buf[b, h] - m_buf[h])
                s_buf[b, h] = probs
                probs_bf = probs.astype(BF16)
                o_buf[h] += dot(kv[b, h, 1], probs_bf, TN)
                return dot(probs_bf, gs[h], NN)

            loop(0, me, lambda b: emit(b, h, 1, value_part(b)))
            acc[h, 1] = value_part(me)
            if h + 1 < heads:
                relay(h + 1)

            rounded = o_buf[h].astype(BF16).astype(F32)
            l_buf[h] = jnp.sum(rounded * gt[h], axis=0, keepdims=True)

            def key_part(b):
                score_grad = (s_buf[b, h] * (dp_buf[b, h] - l_buf[h])).astype(BF16)
                dq_buf[h] += dot(kv[b, h, 0], score_grad, TN)
                return dot(score_grad, qs[h], NN)

            loop(0, me, lambda b: emit(b, h, 0, key_part(b)))
            acc[h, 0] = key_part(me)

        for h in range(heads):
            for r in range(rep):
                part = o_buf[h, :, r * rows : (r + 1) * rows]
                att_ref[:, head_cols(h * rep + r)] = part.T.astype(BF16)
                part = dq_buf[h, :, r * rows : (r + 1) * rows] * SCALE
                dq_ref[:, head_cols(h * rep + r)] = part.T.astype(BF16)
        results[0].start()
        results[1].start()

        for h in range(heads):
            for kind in (1, 0):

                def add(x):
                    src = n - 1 - x
                    down(src, me, h, kind).wait_recv()
                    acc[h, kind] += inb[src, h, kind].astype(F32)

                loop(0, n - 1 - me, add)
                if kind == 1:
                    dv_ref[:, head_cols(h)] = acc[h, 1].astype(BF16)
                else:
                    dk_ref[:, head_cols(h)] = (acc[h, 0] * SCALE).astype(BF16)

        results[2].start()
        results[3].start()

        for h in range(heads):
            loop(skip, n - 1 - me, lambda x: up(me, n - 1 - x, h).wait_send())
            if relayed and me == 2:
                forward(h).wait_send()
            for kind in (1, 0):
                loop(0, me, lambda b: down(me, b, h, kind).wait_send())
        for copy in results:
            copy.wait()

    if n <= 4:
        for i in range(n):
            pl.when(me == i)(functools.partial(run, i))
    else:
        run(me)


def write_out(*refs):
    count = 4
    sources, targets, held = refs[:count], refs[count : 2 * count], refs[2 * count : 3 * count]
    sems = refs[3 * count]
    arriving = [
        pltpu.make_async_copy(sources[i], held[i], sems.at[0, i]) for i in range(count)
    ]
    leaving = [pltpu.make_async_copy(held[i], targets[i], sems.at[1, i]) for i in range(count)]
    for copy in arriving:
        copy.start()
    for i in range(count):
        arriving[i].wait()
        leaving[i].start()
    for copy in leaving:
        copy.wait()


def per_device(queries, keys, values, output_gradient, doc_tiles):
    n = lax.axis_size("seq")
    rows, width = queries.shape
    heads = keys.shape[1] // HEAD_SIZE
    rep = width // keys.shape[1]
    stacked = rows * rep
    hbm = pl.BlockSpec(memory_space=pltpu.HBM)
    block = (n, heads, 2, rows, HEAD_SIZE)
    shapes = (
        jax.ShapeDtypeStruct(queries.shape, BF16),
        jax.ShapeDtypeStruct(queries.shape, BF16),
        jax.ShapeDtypeStruct(keys.shape, BF16),
        jax.ShapeDtypeStruct(keys.shape, BF16),
    )
    dma = pltpu.SemaphoreType.DMA
    results = pl.pallas_call(
        functools.partial(kernel, n),
        out_shape=shapes,
        in_specs=[hbm] * 5,
        out_specs=(hbm,) * 4,
        scratch_shapes=[
            pltpu.VMEM(queries.shape, BF16),
            pltpu.VMEM(queries.shape, BF16),
            pltpu.VMEM(keys.shape, BF16),
            pltpu.VMEM(keys.shape, BF16),
            pltpu.SMEM(doc_tiles.shape, jnp.int32),
            pltpu.VMEM(block, BF16),
            pltpu.VMEM((heads, stacked, HEAD_SIZE), BF16),
            pltpu.VMEM((heads, stacked, HEAD_SIZE), BF16),
            pltpu.VMEM((heads, HEAD_SIZE, stacked), F32),
            pltpu.VMEM((n, heads, rows, stacked), F32),
            pltpu.VMEM((n, heads, rows, stacked), F32),
            pltpu.VMEM((heads, 1, stacked), F32),
            pltpu.VMEM((heads, 1, stacked), F32),
            pltpu.VMEM((heads, HEAD_SIZE, stacked), F32),
            pltpu.VMEM((heads, HEAD_SIZE, stacked), F32),
            pltpu.VMEM((heads, 2, rows, HEAD_SIZE), F32),
            pltpu.VMEM(block, BF16),
            pltpu.VMEM(block, BF16),
            dma,
            dma((heads, 2)),
            dma((heads, rep, 2)),
            dma((n, heads)),
            dma((n, heads)),
            dma((n, heads, 2)),
            dma((n, heads, 2)),
            dma((4,)),
        ],
        compiler_params=pltpu.CompilerParams(
            collective_id=0, has_side_effects=True, vmem_limit_bytes=VMEM_BYTES
        ),
        cost_estimate=pl.CostEstimate(
            flops=12 * n * heads * rows * stacked * HEAD_SIZE,
            bytes_accessed=8 * rows * width,
            transcendentals=2 * n * heads * rows * stacked,
        ),
    )(doc_tiles, queries, keys, values, output_gradient)
    return pl.pallas_call(
        write_out,
        out_shape=shapes,
        in_specs=[hbm] * 4,
        out_specs=(hbm,) * 4,
        scratch_shapes=[pltpu.VMEM(shape.shape, BF16) for shape in shapes] + [dma((2, 4))],
        compiler_params=pltpu.CompilerParams(vmem_limit_bytes=VMEM_BYTES),
    )(*results)


def solution(mesh):
    rows = P(("grp", "seq"), "sub")
    return jax.shard_map(
        per_device,
        mesh=mesh,
        in_specs=(rows, rows, rows, rows, P("grp")),
        out_specs=(rows, rows, rows, rows),
        check_vma=False,
    )
```
